32 devices in a mesh: frame: 8 (over z, x), tile: 4 (over y, core).
Axes of the slice: x: 2, y: 2, z: 4, core: 2. Of those that a mesh axis runs over, the one named last changes fastest.
Arguments:
- frames: bfloat16 [8, 3, 64, 64, 256], P('frame', None, None, 'tile'), may hold values from -6 to 6
- state_in: bfloat16 [8, 64, 64, 256], P('frame', None, 'tile'), may hold values from -6 to 6
- motion: int32 [3, 8, 3, 64], replicated, may hold values from -4 to 63, as said below
- merge_w: bfloat16 [64, 1152], replicated, may hold values from -0.1875 to 0.1875
- res_w: bfloat16 [1, 2, 64, 576], replicated, may hold values from -0.25 to 0.25
Outputs:
- states: bfloat16 [8, 3, 64, 64, 256], P('frame', None, None, 'tile')
The draws below stay inside these ranges and needn't reach their ends.
Inputs may be any that keep to these rules, and one draw needn't show every extreme that they name: motion[0] names a source block of the same frame; blocks t * 16 to t * 16 + 15 form tile owner t. For each section, tick and owner, at most 8 of the owner's 16 destination blocks read blocks of any one owner, and exactly 8 read one owner. motion[1] and motion[2] lie in -4 to 4.
All inputs are finite; a program needn't handle non-finite values.
Results may differ from the reference program's by a relative error of at most 0.0095.
Values may be sent and summed in bfloat16 or wider, within the bound.
No kernel may reach another device: no remote copies, remote signals or barrier semaphores. Data moves between devices by JAX's collectives and lax.ppermute only.
A program may use at most 64 MiB of HBM per device.

```python
import jax
import jax.numpy as jnp
from jax import lax

C = 64
BH = 8
BW = 32
OFF = 4
TICKS = 3
RB = 1
TPD = 16
CAP = 8
TILES = 64
N_FRAME = 8
N_TILE = 4


def draw_motion(key, part):
    base_key = jax.random.fold_in(key, 7)
    k_first, k_pool, k_order, k_block, k_down, k_right = jax.random.split(base_key, 6)
    row_count = N_FRAME * TICKS * N_TILE
    pool_width = (N_TILE - 1) * CAP
    first_owner = jax.random.randint(k_first, (row_count, 1), 0, N_TILE, dtype=jnp.int32)
    others = (first_owner + 1 + jnp.arange(pool_width, dtype=jnp.int32)[None, :] // CAP) % N_TILE
    scores = jax.random.randint(k_pool, (row_count, pool_width), 0, 1 << 20, dtype=jnp.int32) * pool_width + jnp.arange(pool_width, dtype=jnp.int32)[None, :]
    pool_order = jnp.argsort(scores, axis=1)
    picked = jnp.take_along_axis(others, pool_order, axis=1)[:, :TPD - CAP]
    owners = jnp.concatenate([jnp.broadcast_to(first_owner, (row_count, CAP)), picked], axis=1)
    mixing = jax.random.randint(k_order, (row_count, TPD), 0, 1 << 20, dtype=jnp.int32) * TPD + jnp.arange(TPD, dtype=jnp.int32)[None, :]
    owners = jnp.take_along_axis(owners, jnp.argsort(mixing, axis=1), axis=1)
    local_block = jax.random.randint(k_block, (row_count, TPD), 0, TPD, dtype=jnp.int32)
    source = (owners * TPD + local_block).reshape(N_FRAME, TICKS, N_TILE * TPD)
    down_by = jax.random.randint(k_down, (N_FRAME, TICKS, N_TILE * TPD), -OFF, OFF + 1, dtype=jnp.int32)
    right_by = jax.random.randint(k_right, (N_FRAME, TICKS, N_TILE * TPD), -OFF, OFF + 1, dtype=jnp.int32)
    return jnp.stack([source, down_by, right_by]).astype(jnp.int32)


def level_of(key, extent, cuts, low, top_value):
    def one(axis_at, shards_of):
        steps = jax.random.uniform(jax.random.fold_in(jax.random.fold_in(key, 6), axis_at), (shards_of,), jnp.float32, low / len(cuts), top_value / len(cuts))
        return jnp.repeat(jnp.exp(steps), extent[axis_at] // shards_of).reshape((-1,) + (1,) * (len(extent) - axis_at - 1))

    factor_of = one(*cuts[0])
    for cut in cuts[1:]:
        factor_of = factor_of * one(*cut)
    return factor_of


def normal_values(stream_key, shape, deviation, limit, cuts=(), kind=jnp.bfloat16):
    values = deviation * jax.random.normal(stream_key, shape, jnp.float32)
    if cuts:
        values = values * level_of(stream_key, shape, cuts, -0.22, 0.18)
    return jnp.clip(values, -limit, limit).astype(kind)


def setup_inputs(seed: int = 0) -> dict:
    seeds = jax.random.split(jax.random.key(seed), 6)
    return {
        "frames": normal_values(seeds[0], (N_FRAME, TICKS, C, TILES, BH * BW), 1.0, 6.0, ((0, 8), (3, 4))),
        "state_in": normal_values(seeds[1], (N_FRAME, C, TILES, BH * BW), 1.0, 6.0, ((0, 8), (2, 4))),
        "motion": draw_motion(jax.random.fold_in(seeds[5], 71), 0),
        "merge_w": normal_values(seeds[3], (C, 18 * C), (18 * C) ** -0.5, 0.1875),
        "res_w": normal_values(seeds[4], (RB, 2, C, 9 * C), (9 * C) ** -0.5, 0.25),
    }


def displace(field, down_by, right_by, keep):
    pixels = field.shape[-1]
    padding = OFF * (BW + 1)
    widths = [(0, 0)] * (field.ndim - 1) + [(padding, padding)]
    padded = jnp.pad(field, widths)
    window = lax.dynamic_slice_in_dim(padded, padding + down_by * BW + right_by, pixels, field.ndim - 1)
    places = jnp.arange(pixels, dtype=jnp.int32)
    row_at = places // BW + down_by
    col_at = places % BW + right_by
    inside = (row_at >= 0) & (row_at < pixels // BW) & (col_at >= 0) & (col_at < BW) & keep
    return jnp.where(inside, window, jnp.zeros_like(window))


def convolve(field, kernel):
    in_width, count, pixels = field.shape
    taps = [displace(field, row_step, col_step, True) for row_step in (-1, 0, 1) for col_step in (-1, 0, 1)]
    stacked = jnp.stack(taps).reshape(9 * in_width, count * pixels)
    result = jnp.dot(kernel, stacked, preferred_element_type=jnp.float32)
    return result.reshape(kernel.shape[0], count, pixels)


def advance(warped, frame_now, merge_w, res_w):
    joined = jnp.concatenate([frame_now, warped], axis=0)
    merged = convolve(joined, merge_w)
    merged = jnp.where(merged > 0, merged, 0.1 * merged).astype(jnp.bfloat16)
    hidden = merged
    for layer_index in range(res_w.shape[0]):
        middle = jax.nn.relu(convolve(hidden, res_w[layer_index, 0])).astype(jnp.bfloat16)
        hidden = (hidden.astype(jnp.float32) + convolve(middle, res_w[layer_index, 1])).astype(jnp.bfloat16)
    return hidden


def one_section(packed):
    previous, frame_now, columns, merge_w, res_w = packed
    blocks = jnp.take(previous, columns[0], axis=1)
    warped = jax.vmap(displace, in_axes=(1, 0, 0, None), out_axes=1)(blocks, columns[1], columns[2], True)
    return advance(warped, frame_now, merge_w, res_w)


def reference(frames, state_in, motion, merge_w, res_w):
    previous = state_in
    outputs = []
    for tick_index in range(TICKS):
        columns = jnp.transpose(motion[:, :, tick_index, :], (1, 0, 2))

        def section_work(packed):
            return one_section((packed[0], packed[1], packed[2], merge_w, res_w))

        produced = lax.map(section_work, (previous, frames[:, tick_index], columns))
        outputs.append(produced)
        previous = jnp.roll(produced, 1, axis=0)
    return jnp.stack(outputs, axis=1)
```

```python
import functools

import jax
import jax.numpy as jnp
from jax import lax
from jax.experimental import pallas as pl
from jax.experimental.pallas import tpu as pltpu
from jax.sharding import PartitionSpec as P

BW = 32
F32 = jnp.float32
BF16 = jnp.bfloat16
VMEM_LIMIT = 48 * 1024 * 1024


def lanes_of(pixels):
    return lax.broadcasted_iota(jnp.int32, (1, pixels), 1)


def column_taps(field):
    pixels = field.shape[-1]
    col = lanes_of(pixels) % BW
    zero = jnp.zeros_like(field)
    left = jnp.where(col != 0, pltpu.roll(field, 1, 1), zero)
    right = jnp.where(col != BW - 1, pltpu.roll(field, pixels - 1, 1), zero)
    return jnp.concatenate([left, field, right], axis=0)


def sum_rows(parts):
    channels, pixels = parts.shape[0] // 3, parts.shape[1]
    lane = lanes_of(pixels)
    up = jnp.where(lane >= BW, pltpu.roll(parts[:channels], BW, 1), 0.0)
    down = jnp.where(lane < pixels - BW, pltpu.roll(parts[2 * channels :], pixels - BW, 1), 0.0)
    return parts[channels : 2 * channels] + up + down


def conv_block(field, weight):
    return sum_rows(jnp.dot(weight, column_taps(field), preferred_element_type=F32))


def displaced(block, down_by, right_by):
    pixels = block.shape[-1]
    lane = lanes_of(pixels)
    row_at = lane // BW + down_by
    col_at = lane % BW + right_by
    inside = (row_at >= 0) & (row_at < pixels // BW) & (col_at >= 0) & (col_at < BW)
    turn = lax.rem(2 * pixels - (down_by * BW + right_by), pixels)
    moved = pltpu.roll(block, turn, 1)
    return jnp.where(inside, moved, jnp.zeros_like(moved))


def send_table(source_of, owner_now, tiles, per_owner, slots, table):
    for at in range((tiles - 1) * slots):
        table[at] = 0
    for j in range(1, tiles):
        first = (owner_now ^ j) * per_owner

        def step(g, used):
            source = source_of(first + g)
            mine = source // per_owner == owner_now

            @pl.when(mine)
            def _():
                table[(j - 1) * slots + used] = source % per_owner

            return jnp.where(mine, used + 1, used)

        lax.fori_loop(0, per_owner, step, jnp.int32(0))


def read_table(source_of, owner_now, tiles, per_owner, slots, counts, table):
    for j in range(tiles):
        counts[j] = 0
    for g in range(per_owner):
        source = source_of(owner_now * per_owner + g)
        j = (source // per_owner) ^ owner_now
        used = counts[j]
        counts[j] = used + 1
        table[g] = jnp.where(
            j == 0, source % per_owner, per_owner + (j - 1) * slots + jnp.minimum(used, slots - 1)
        )


def fetch_motion(motion, section, tick, scratch, sem):
    copy = pltpu.make_async_copy(motion.at[:, section], scratch, sem)
    copy.start()
    copy.wait()
    return lambda column, block: scratch[column, tick, block]


def first_kernel(tiles, slots, motion, state, own, *rest):
    sends, (motion_here, sem, table) = rest[: tiles - 1], rest[tiles - 1 :]
    per_owner = own.shape[0]
    owner_now = lax.axis_index("tile")
    read = fetch_motion(motion, lax.axis_index("frame"), 0, motion_here, sem)
    own[...] = jnp.swapaxes(state[...], 0, 1)
    send_table(lambda b: read(0, b), owner_now, tiles, per_owner, slots, table)
    for j in range(1, tiles):
        for s in range(slots):
            sends[j - 1][s] = own[table[(j - 1) * slots + s]]


def frame_kernel(tiles, slots, tick, motion, frame, weight, part, reads, sends, motion_here, sem, counts):
    per_owner = part.shape[0]
    owner_now = lax.axis_index("tile")
    count = lax.axis_size("frame")
    section = lax.axis_index("frame")
    here = lax.rem(section + tick, count)
    read = fetch_motion(motion, here, tick, motion_here, sem)
    read_table(lambda b: read(0, b), owner_now, tiles, per_owner, slots, counts, reads)
    for g in range(per_owner):
        reads[per_owner + g] = read(1, owner_now * per_owner + g)
        reads[2 * per_owner + g] = read(2, owner_now * per_owner + g)
    if tick + 1 < motion.shape[2]:
        ahead = fetch_motion(motion, lax.rem(section + tick + 1, count), tick + 1, motion_here, sem)
        send_table(lambda b: ahead(0, b), owner_now, tiles, per_owner, slots, sends)
    blocks = jnp.swapaxes(frame[...], 0, 1)
    for g in range(per_owner):
        part[g] = conv_block(blocks[g], weight[...])


def tick_kernel(tiles, slots, more, reads, sends_at, own, *rest):
    arrived, rest = rest[: tiles - 1], rest[tiles - 1 :]
    part, warp_w, first_w, second_w, hidden, *rest = rest
    sends, (pool, sems) = rest[: len(rest) - 2], rest[len(rest) - 2 :]
    per_owner = part.shape[0]
    copies = [pltpu.make_async_copy(own, pool.at[pl.ds(0, per_owner)], sems.at[0])]
    for j in range(1, tiles):
        start = per_owner + (j - 1) * slots
        copies.append(
            pltpu.make_async_copy(arrived[j - 1], pool.at[pl.ds(start, slots)], sems.at[j])
        )
    for copy in copies:
        copy.start()
    for copy in copies:
        copy.wait()
    group = 4

    def step(at, carry):
        for inner in range(group):
            g = at * group + inner
            warped = displaced(pool[reads[g]], reads[per_owner + g], reads[2 * per_owner + g])
            merged = part[g] + conv_block(warped, warp_w[...])
            merged = jnp.where(merged > 0, merged, 0.1 * merged).astype(BF16)
            middle = jnp.maximum(conv_block(merged, first_w[...]), 0.0).astype(BF16)
            hidden[g] = (merged.astype(F32) + conv_block(middle, second_w[...])).astype(BF16)
        return carry

    lax.fori_loop(0, per_owner // group, step, 0)
    if more:
        for j in range(1, tiles):
            for s in range(slots):
                sends[j - 1][s] = hidden[sends_at[(j - 1) * slots + s]]


def place_kernel(tick, blocks, *rest):
    out, turned, sem = rest[-3:]
    turned[...] = jnp.swapaxes(blocks[...], 0, 1)
    copy = pltpu.make_async_copy(turned, out.at[0, tick], sem)
    copy.start()
    copy.wait()


def spec(space):
    return pl.BlockSpec(memory_space=space)


def params():
    return pltpu.CompilerParams(vmem_limit_bytes=VMEM_LIMIT)


def along(value, axis, steps):
    count = lax.axis_size(axis)
    return lax.ppermute(value, axis, [(s, (s + steps) % count) for s in range(count)])


def across_tiles(sends):
    count = lax.axis_size("tile")
    return [
        lax.ppermute(value, "tile", [(s, s ^ (j + 1)) for s in range(count)])
        for j, value in enumerate(sends)
    ]


def by_rows(weight, taken):
    out_width = weight.shape[0]
    split = weight.reshape(out_width, 3, 3, -1)[..., taken]
    return split.transpose(1, 0, 2, 3).reshape(3 * out_width, -1)


def per_device(frames, state_in, motion, merge_w, res_w):
    tiles = lax.axis_size("tile")
    _, ticks, channels, per_owner, pixels = frames.shape
    slots = max(2, 2 * per_owner // tiles)
    motion_rows = (motion.shape[0], *motion.shape[2:])
    block_shape = (per_owner, channels, pixels)
    slot_shape = (slots, channels, pixels)
    frame_w = by_rows(merge_w, slice(0, channels))
    warp_w = by_rows(merge_w, slice(channels, None))
    first_w = by_rows(res_w[0, 0], slice(None))
    second_w = by_rows(res_w[0, 1], slice(None))
    hbm, vmem, smem = pl.ANY, pltpu.VMEM, pltpu.SMEM
    blocks_out = jax.ShapeDtypeStruct(block_shape, BF16)
    slots_out = [jax.ShapeDtypeStruct(slot_shape, BF16)] * (tiles - 1)
    motion_scratch = [pltpu.SMEM(motion_rows, jnp.int32), pltpu.SemaphoreType.DMA]

    brought = [frames[0, 0]] + [along(frames[0, k], "frame", -k) for k in range(1, ticks)]
    own, *sends = pl.pallas_call(
        functools.partial(first_kernel, tiles, slots),
        out_shape=[blocks_out, *slots_out],
        in_specs=[spec(hbm), spec(vmem)],
        out_specs=[spec(vmem)] * tiles,
        scratch_shapes=[*motion_scratch, pltpu.SMEM(((tiles - 1) * slots,), jnp.int32)],
        compiler_params=params(),
    )(motion, state_in[0])
    result = None
    for tick in range(ticks):
        arrived = across_tiles(sends)
        part, reads, sends_at = pl.pallas_call(
            functools.partial(frame_kernel, tiles, slots, tick),
            out_shape=[
                jax.ShapeDtypeStruct(block_shape, F32),
                jax.ShapeDtypeStruct((3 * per_owner,), jnp.int32),
                jax.ShapeDtypeStruct(((tiles - 1) * slots,), jnp.int32),
            ],
            in_specs=[spec(hbm), spec(vmem), spec(vmem)],
            out_specs=[spec(vmem), spec(smem), spec(smem)],
            scratch_shapes=[*motion_scratch, pltpu.SMEM((tiles,), jnp.int32)],
            compiler_params=params(),
            cost_estimate=pl.CostEstimate(
                flops=2 * 9 * channels * channels * per_owner * pixels,
                bytes_accessed=8 * per_owner * channels * pixels,
                transcendentals=0,
            ),
        )(motion, brought[tick], frame_w)
        more = tick + 1 < ticks
        hidden, *sends = pl.pallas_call(
            functools.partial(tick_kernel, tiles, slots, more),
            out_shape=[blocks_out, *(slots_out if more else [])],
            in_specs=[spec(smem)] * 2 + [spec(hbm)] * tiles + [spec(vmem)] * 4,
            out_specs=[spec(vmem)] * (tiles if more else 1),
            scratch_shapes=[
                pltpu.VMEM((per_owner + (tiles - 1) * slots, channels, pixels), BF16),
                pltpu.SemaphoreType.DMA((tiles,)),
            ],
            compiler_params=params(),
        )(reads, sends_at, own, *arrived, part, warp_w, first_w, second_w)
        own = hidden
        home = along(hidden, "frame", tick) if tick else hidden
        result = pl.pallas_call(
            functools.partial(place_kernel, tick),
            out_shape=jax.ShapeDtypeStruct(frames.shape, BF16),
            in_specs=[spec(vmem)] + ([spec(hbm)] if tick else []),
            out_specs=spec(hbm),
            scratch_shapes=[
                pltpu.VMEM((channels, per_owner, pixels), BF16),
                pltpu.SemaphoreType.DMA,
            ],
            input_output_aliases={1: 0} if tick else {},
            compiler_params=params(),
        )(home, *([result] if tick else []))
    return result


def solution(mesh):
    placed = (P("frame", None, None, "tile", None), P("frame", None, "tile", None), P(), P(), P())
    return jax.shard_map(
        per_device,
        mesh=mesh,
        in_specs=placed,
        out_specs=P("frame", None, None, "tile", None),
        check_vma=False,
    )
```

```python
import functools

import jax
import jax.numpy as jnp
from jax import lax
from jax.experimental import pallas as pl
from jax.experimental.pallas import tpu as pltpu
from jax.sharding import PartitionSpec as P

BW = 32
LANES = 128
F32 = jnp.float32
BF16 = jnp.bfloat16
VMEM_LIMIT = 48 * 1024 * 1024
GROUP = 4


def lane_ids():
    return lax.broadcasted_iota(jnp.int32, (1, LANES), 1)


def turned(field, by):
    by = by % LANES
    return pltpu.roll(field, by, field.ndim - 1) if by else field


def by_quarter(pieces):
    quarter = lane_ids() // BW
    out = pieces[0]
    for q in range(1, len(pieces)):
        out = jnp.where(quarter == q, pieces[q], out)
    return out


def split_rows(field):
    top, low = field[..., :LANES], field[..., LANES:]
    even = by_quarter([top, turned(top, -BW), turned(low, 2 * BW), turned(low, BW)])
    odd = by_quarter([turned(top, -BW), turned(top, -2 * BW), turned(low, BW), low])
    return even, odd


def join_rows(even, odd):
    top = by_quarter([even, turned(odd, BW), turned(even, BW), turned(odd, 2 * BW)])
    low = by_quarter([turned(even, -2 * BW), turned(odd, -BW), turned(even, -BW), odd])
    return top, low


def kept(mask):
    return jnp.where(mask, 1.0, 0.0).astype(BF16)


def column_taps(half):
    col = lane_ids() % BW
    left = turned(half, 1) * kept(col != 0)
    right = turned(half, -1) * kept(col != BW - 1)
    return jnp.concatenate([left, half, right], axis=0)


def conv_block(even, odd, weight):
    stacked = jnp.concatenate([column_taps(even), column_taps(odd)], axis=1)
    parts = jnp.dot(weight, stacked, preferred_element_type=F32)
    width = parts.shape[0] // 3
    above, here, below = (parts[a * width : (a + 1) * width] for a in range(3))
    lane = lane_ids()
    from_odd = jnp.where(lane >= BW, turned(above[:, LANES:], BW), 0.0)
    from_even = jnp.where(lane < LANES - BW, turned(below[:, :LANES], -BW), 0.0)
    even_out = here[:, :LANES] + below[:, LANES:] + from_odd
    odd_out = here[:, LANES:] + above[:, :LANES] + from_even
    return even_out, odd_out


def displaced(block, down_by, right_by):
    lane = lane_ids()
    odd_step = down_by & 1
    col_at = lane % BW + right_by
    col_ok = (col_at >= 0) & (col_at < BW)
    out = []
    for half in range(2):
        row_at = 2 * (lane // BW) + half + down_by
        inside = (row_at >= 0) & (row_at < 2 * (LANES // BW)) & col_ok
        steps = (down_by + half) >> 1
        turn = (4 * LANES - (steps * BW + right_by)) & (LANES - 1)
        source = block[odd_step ^ half]
        out.append(pltpu.roll(source, turn, 1) * kept(inside))
    return out


def send_table(source_of, owner_now, tiles, per_owner, slots, table):
    for at in range((tiles - 1) * slots):
        table[at] = 0
    for j in range(1, tiles):
        first = (owner_now ^ j) * per_owner

        def step(g, used):
            source = source_of(first + g)
            mine = source // per_owner == owner_now

            @pl.when(mine)
            def _():
                table[(j - 1) * slots + used] = source % per_owner

            return jnp.where(mine, used + 1, used)

        lax.fori_loop(0, per_owner, step, jnp.int32(0))


def read_table(source_of, owner_now, tiles, per_owner, slots, counts, table):
    for j in range(tiles):
        counts[j] = 0
    for g in range(per_owner):
        source = source_of(owner_now * per_owner + g)
        j = (source // per_owner) ^ owner_now
        used = counts[j]
        counts[j] = used + 1
        table[g] = j
        table[per_owner + g] = jnp.where(j == 0, source % per_owner, jnp.minimum(used, slots - 1))


def fetch_motion(motion, section, tick, scratch, sem):
    copy = pltpu.make_async_copy(motion.at[:, tick], scratch, sem)
    copy.start()
    copy.wait()
    return lambda column, block: scratch[column, section, block]


def send_slots(blocks, table, sends, slots, sems):
    copies = [
        pltpu.make_async_copy(
            blocks.at[table[j * slots + s]], send.at[s], sems.at[j * slots + s]
        )
        for j, send in enumerate(sends)
        for s in range(slots)
    ]
    for copy in copies:
        copy.start()
    return copies


def first_kernel(tiles, slots, motion, state, own, *rest):
    sends, (motion_here, sem, table, sems) = rest[: tiles - 1], rest[tiles - 1 :]
    per_owner = own.shape[0]
    owner_now = lax.axis_index("tile")
    read = fetch_motion(motion, lax.axis_index("frame"), 0, motion_here, sem)
    send_table(lambda b: read(0, b), owner_now, tiles, per_owner, slots, table)
    even, odd = split_rows(jnp.swapaxes(state[...], 0, 1))
    own[:, 0] = even
    own[:, 1] = odd
    for copy in send_slots(own, table, sends, slots, sems):
        copy.wait()


def weight_kernel(merge, res, frame_w, warp_w, first_w, second_w):
    width = merge.shape[0]
    for a in range(3):
        rows = slice(a * width, (a + 1) * width)
        for out, layer in ((first_w, 0), (second_w, 1)):
            out[rows] = res[0, layer, :, 3 * a * width : 3 * (a + 1) * width]
        for out, which in ((frame_w, 0), (warp_w, 1)):
            starts = [(2 * (3 * a + b) + which) * width for b in range(3)]
            out[rows] = jnp.concatenate([merge[:, s : s + width] for s in starts], axis=1)


def frame_kernel(tiles, slots, tick, motion, frames, weight, part, reads, sends, *scratch):
    motion_here, sem, counts, frame, frame_sem = scratch
    copy = pltpu.make_async_copy(frames.at[0, tick] if tick == 0 else frames, frame, frame_sem)
    copy.start()
    per_owner = part.shape[0]
    owner_now = lax.axis_index("tile")
    count = lax.axis_size("frame")
    section = lax.axis_index("frame")
    read = fetch_motion(motion, lax.rem(section + tick, count), tick, motion_here, sem)
    read_table(lambda b: read(0, b), owner_now, tiles, per_owner, slots, counts, reads)
    for g in range(per_owner):
        reads[2 * per_owner + g] = read(1, owner_now * per_owner + g)
        reads[3 * per_owner + g] = read(2, owner_now * per_owner + g)
    if tick + 1 < motion.shape[1]:
        ahead = fetch_motion(motion, lax.rem(section + tick + 1, count), tick + 1, motion_here, sem)
        send_table(lambda b: ahead(0, b), owner_now, tiles, per_owner, slots, sends)
    copy.wait()
    even, odd = split_rows(jnp.swapaxes(frame[...], 0, 1))
    for g in range(per_owner):
        part[g, 0], part[g, 1] = conv_block(even[g], odd[g], weight[...])


def tick_kernel(tiles, slots, more, reads, sends_at, *rest):
    pools, rest = rest[:tiles], rest[tiles:]
    part, warp_w, first_w, second_w, hidden, *rest = rest
    sends, (blocks, sems, send_sems) = rest[: len(rest) - 3], rest[len(rest) - 3 :]
    per_owner = part.shape[0]
    for g in range(per_owner):
        for j in range(tiles):

            @pl.when(reads[g] == j)
            def _():
                pltpu.make_async_copy(
                    pools[j].at[reads[per_owner + g]], blocks.at[g], sems.at[g]
                ).start()

    for g in range(per_owner):
        pltpu.make_async_copy(pools[0].at[0], blocks.at[g], sems.at[g]).wait()
    merged, middle = {}, {}

    def merge(g):
        warped = displaced(blocks.at[g], reads[2 * per_owner + g], reads[3 * per_owner + g])
        sums = conv_block(*warped, warp_w[...])
        sums = [part[g, h] + sums[h] for h in range(2)]
        merged[g] = [jnp.where(v > 0, v, 0.1 * v).astype(BF16) for v in sums]

    def first(g):
        middle[g] = [
            jnp.maximum(v, 0.0).astype(BF16) for v in conv_block(*merged[g], first_w[...])
        ]

    def second(g):
        sums = conv_block(*middle[g], second_w[...])
        for h in range(2):
            hidden[g, h] = (merged[g][h].astype(F32) + sums[h]).astype(BF16)

    stages = (merge, first, second)
    groups = per_owner // GROUP
    for step in range(groups + len(stages) - 1):
        for at in reversed(range(len(stages))):
            if 0 <= step - at < groups:
                for g in range((step - at) * GROUP, (step - at + 1) * GROUP):
                    stages[at](g)
    if more:
        for copy in send_slots(hidden, sends_at, sends, slots, send_sems):
            copy.wait()


def place_kernel(tick, blocks, *rest):
    out, laid, sem = rest[-3:]
    top, low = join_rows(blocks[:, 0], blocks[:, 1])
    laid[...] = jnp.swapaxes(jnp.concatenate([top, low], axis=-1), 0, 1)
    copy = pltpu.make_async_copy(laid, out.at[0, tick], sem)
    copy.start()
    copy.wait()


def spec(space):
    return pl.BlockSpec(memory_space=space)


def params():
    return pltpu.CompilerParams(vmem_limit_bytes=VMEM_LIMIT)


def along(value, axis, steps):
    count = lax.axis_size(axis)
    return lax.ppermute(value, axis, [(s, (s + steps) % count) for s in range(count)])


def across_tiles(sends):
    count = lax.axis_size("tile")
    return [
        lax.ppermute(value, "tile", [(s, s ^ (j + 1)) for s in range(count)])
        for j, value in enumerate(sends)
    ]


def per_device(frames, state_in, motion, merge_w, res_w):
    tiles = lax.axis_size("tile")
    _, ticks, channels, per_owner, pixels = frames.shape
    slots = max(2, 2 * per_owner // tiles)
    block = (2, channels, pixels // 2)
    hbm, vmem, smem = pl.ANY, pltpu.VMEM, pltpu.SMEM
    motion = motion.transpose(0, 2, 1, 3)
    blocks_out = jax.ShapeDtypeStruct((per_owner, *block), BF16)
    slots_out = [jax.ShapeDtypeStruct((slots, *block), BF16)] * (tiles - 1)
    slot_count = (tiles - 1) * slots
    motion_scratch = [
        pltpu.SMEM((motion.shape[0], *motion.shape[2:]), jnp.int32),
        pltpu.SemaphoreType.DMA,
    ]
    sends_space = [spec(hbm)] * (tiles - 1)

    own, *sends = pl.pallas_call(
        functools.partial(first_kernel, tiles, slots),
        out_shape=[blocks_out, *slots_out],
        in_specs=[spec(hbm), spec(vmem)],
        out_specs=[spec(vmem), *sends_space],
        scratch_shapes=[
            *motion_scratch,
            pltpu.SMEM((slot_count,), jnp.int32),
            pltpu.SemaphoreType.DMA((slot_count,)),
        ],
        compiler_params=params(),
    )(motion, state_in[0])
    square = jax.ShapeDtypeStruct((3 * channels, 3 * channels), BF16)
    frame_w, warp_w, first_w, second_w = pl.pallas_call(
        weight_kernel,
        out_shape=[square] * 4,
        in_specs=[spec(vmem)] * 2,
        out_specs=[spec(vmem)] * 4,
        compiler_params=params(),
    )(merge_w, res_w)
    brought = [frames] + [along(frames[0, k], "frame", -k) for k in range(1, ticks)]
    result = None
    for tick in range(ticks):
        arrived = across_tiles(sends)
        part, reads, sends_at = pl.pallas_call(
            functools.partial(frame_kernel, tiles, slots, tick),
            out_shape=[
                jax.ShapeDtypeStruct((per_owner, *block), F32),
                jax.ShapeDtypeStruct((4 * per_owner,), jnp.int32),
                jax.ShapeDtypeStruct((slot_count,), jnp.int32),
            ],
            in_specs=[spec(hbm), spec(hbm), spec(vmem)],
            out_specs=[spec(vmem), spec(smem), spec(smem)],
            scratch_shapes=[
                *motion_scratch,
                pltpu.SMEM((tiles,), jnp.int32),
                pltpu.VMEM((channels, per_owner, pixels), BF16),
                pltpu.SemaphoreType.DMA,
            ],
            compiler_params=params(),
            cost_estimate=pl.CostEstimate(
                flops=2 * 9 * channels * channels * per_owner * pixels,
                bytes_accessed=8 * per_owner * channels * pixels,
                transcendentals=0,
            ),
        )(motion, brought[tick], frame_w)
        more = tick + 1 < ticks
        hidden, *sends = pl.pallas_call(
            functools.partial(tick_kernel, tiles, slots, more),
            out_shape=[blocks_out, *(slots_out if more else [])],
            in_specs=[spec(smem)] * 2 + [spec(hbm)] * tiles + [spec(vmem)] * 4,
            out_specs=[spec(vmem), *(sends_space if more else [])],
            scratch_shapes=[
                pltpu.VMEM((per_owner, *block), BF16),
                pltpu.SemaphoreType.DMA((per_owner,)),
                pltpu.SemaphoreType.DMA((slot_count,)),
            ],
            compiler_params=params(),
        )(reads, sends_at, own, *arrived, part, warp_w, first_w, second_w)
        own = hidden
        home = along(hidden, "frame", tick) if tick else hidden
        result = pl.pallas_call(
            functools.partial(place_kernel, tick),
            out_shape=jax.ShapeDtypeStruct(frames.shape, BF16),
            in_specs=[spec(vmem)] + ([spec(hbm)] if tick else []),
            out_specs=spec(hbm),
            scratch_shapes=[
                pltpu.VMEM((channels, per_owner, pixels), BF16),
                pltpu.SemaphoreType.DMA,
            ],
            input_output_aliases={1: 0} if tick else {},
            compiler_params=params(),
        )(home, *([result] if tick else []))
    return result


def solution(mesh):
    placed = (P("frame", None, None, "tile", None), P("frame", None, "tile", None), P(), P(), P())
    return jax.shard_map(
        per_device,
        mesh=mesh,
        in_specs=placed,
        out_specs=P("frame", None, None, "tile", None),
        check_vma=False,
    )
```

```python
import functools

import jax
import jax.numpy as jnp
from jax import lax
from jax.experimental import pallas as pl
from jax.experimental.pallas import tpu as pltpu
from jax.sharding import PartitionSpec as P

BW = 32
LANES = 128
F32 = jnp.float32
BF16 = jnp.bfloat16
VMEM_LIMIT = 48 * 1024 * 1024
FULL_VMEM = 63 * 1024 * 1024
GROUP = 4


def lane_ids():
    return lax.broadcasted_iota(jnp.int32, (1, LANES), 1)


def turned(field, by):
    by = by % LANES
    return pltpu.roll(field, by, field.ndim - 1) if by else field


def by_quarter(pieces):
    quarter = lane_ids() // BW
    out = pieces[0]
    for q in range(1, len(pieces)):
        out = jnp.where(quarter == q, pieces[q], out)
    return out


def split_rows(field):
    top, low = field[..., :LANES], field[..., LANES:]
    even = by_quarter([top, turned(top, -BW), turned(low, 2 * BW), turned(low, BW)])
    odd = by_quarter([turned(top, -BW), turned(top, -2 * BW), turned(low, BW), low])
    return even, odd


def join_rows(even, odd):
    top = by_quarter([even, turned(odd, BW), turned(even, BW), turned(odd, 2 * BW)])
    low = by_quarter([turned(even, -2 * BW), turned(odd, -BW), turned(even, -BW), odd])
    return top, low


def kept(mask):
    return jnp.where(mask, 1.0, 0.0).astype(BF16)


def column_taps(half):
    col = lane_ids() % BW
    left = turned(half, 1) * kept(col != 0)
    right = turned(half, -1) * kept(col != BW - 1)
    return jnp.concatenate([left, half, right], axis=0)


def conv_block(even, odd, weight):
    stacked = jnp.concatenate([column_taps(even), column_taps(odd)], axis=1)
    parts = jnp.dot(weight, stacked, preferred_element_type=F32)
    width = parts.shape[0] // 3
    above, here, below = (parts[a * width : (a + 1) * width] for a in range(3))
    lane = lane_ids()
    from_odd = jnp.where(lane >= BW, turned(above[:, LANES:], BW), 0.0)
    from_even = jnp.where(lane < LANES - BW, turned(below[:, :LANES], -BW), 0.0)
    even_out = here[:, :LANES] + below[:, LANES:] + from_odd
    odd_out = here[:, LANES:] + above[:, :LANES] + from_even
    return even_out, odd_out


def displaced(block, down_by, right_by):
    lane = lane_ids()
    odd_step = down_by & 1
    col_at = lane % BW + right_by
    col_ok = (col_at >= 0) & (col_at < BW)
    out = []
    for half in range(2):
        row_at = 2 * (lane // BW) + half + down_by
        inside = (row_at >= 0) & (row_at < 2 * (LANES // BW)) & col_ok
        steps = (down_by + half) >> 1
        turn = (4 * LANES - (steps * BW + right_by)) & (LANES - 1)
        source = block[odd_step ^ half]
        out.append(pltpu.roll(source, turn, 1) * kept(inside))
    return out


def owner_of(block, per_owner):
    return block >> (per_owner.bit_length() - 1)


def place_of(block, per_owner):
    return block & (per_owner - 1)


def send_table(source_of, owner_now, tiles, per_owner, slots, table):
    for at in range((tiles - 1) * (slots + 1)):
        table[at] = 0
    for j in range(1, tiles):
        first = (owner_now ^ j) * per_owner
        used = jnp.int32((j - 1) * (slots + 1))
        for g in range(per_owner):
            source = source_of(first + g)
            table[used] = place_of(source, per_owner)
            last = jnp.int32((j - 1) * (slots + 1) + slots)
            used = jnp.where(owner_of(source, per_owner) == owner_now, jnp.minimum(used + 1, last), used)


def read_table(source_of, owner_now, tiles, per_owner, slots, counts, table):
    for j in range(tiles):
        counts[j] = 0
    for g in range(per_owner):
        source = source_of(owner_now * per_owner + g)
        j = owner_of(source, per_owner) ^ owner_now
        used = counts[j]
        counts[j] = used + 1
        table[g] = j
        table[per_owner + g] = jnp.where(
            j == 0, place_of(source, per_owner), jnp.minimum(used, slots - 1)
        )


def fetch_motion(motion, section, tick, scratch, sem):
    copy = pltpu.make_async_copy(motion.at[:, tick], scratch, sem)
    copy.start()

    def arrived():
        copy.wait()
        return lambda column, block: scratch[column, section, block]

    return arrived


def table_kernel(tiles, slots, tick, ahead, motion, _, reads, sends, motion_here, sem, counts):
    per_owner = reads.shape[0] // 4
    owner_now = lax.axis_index("tile")
    section = lax.rem(lax.axis_index("frame") + ahead, lax.axis_size("frame"))
    read = fetch_motion(motion, section, tick, motion_here, sem)()
    read_table(lambda b: read(0, b), owner_now, tiles, per_owner, slots, counts, reads)
    for g in range(per_owner):
        reads[2 * per_owner + g] = read(1, owner_now * per_owner + g)
        reads[3 * per_owner + g] = read(2, owner_now * per_owner + g)
    send_table(lambda b: read(0, b), owner_now, tiles, per_owner, slots, sends)


def started(copies):
    for copy in copies:
        copy.start()
    return copies


def waited(copies):
    for copy in copies:
        copy.wait()


def send_slots(blocks, table, sends, slots, sems, channels=slice(None)):
    return started(
        [
            pltpu.make_async_copy(
                blocks.at[table[j * (slots + 1) + s], :, channels],
                send.at[s],
                sems.at[j * slots + s],
            )
            for j, send in enumerate(sends)
            for s in range(slots)
        ]
    )


def gather_blocks(pools, reads, into, sems):
    per_owner = reads.shape[0] // 4
    for g in range(per_owner):
        for j, (pool, channels) in enumerate(pools):

            @pl.when(reads[g] == j)
            def _():
                source = pool.at[reads[per_owner + g], :, channels]
                pltpu.make_async_copy(source, into(g), sems.at[g]).start()

    pool, channels = pools[0]
    return [
        pltpu.make_async_copy(pool.at[0, :, channels], into(g), sems.at[g])
        for g in range(per_owner)
    ]


def first_kernel(tiles, slots, motion, state, own, token, *rest):
    token[0] = 0
    sends, (motion_here, sem, table, sems, raw, raw_sems) = rest[: tiles - 1], rest[tiles - 1 :]
    per_owner, _, channels = own.shape[:3]
    owner_now = lax.axis_index("tile")
    arrived = fetch_motion(motion, lax.axis_index("frame"), 0, motion_here, sem)
    chunk = channels // 4
    copies = started(
        [
            pltpu.make_async_copy(
                state.at[0, pl.ds(i * chunk, chunk)], raw.at[pl.ds(i * chunk, chunk)], raw_sems.at[i]
            )
            for i in range(4)
        ]
    )
    read = arrived()
    send_table(lambda b: read(0, b), owner_now, tiles, per_owner, slots, table)
    for i, copy in enumerate(copies):
        copy.wait()
        at = slice(i * chunk, (i + 1) * chunk)
        even, odd = split_rows(jnp.swapaxes(raw[at], 0, 1))
        own[:, 0, at] = even
        own[:, 1, at] = odd
    waited(send_slots(own, table, sends, slots, sems))


def weight_kernel(merge, res, _, frame_w, warp_w, first_w, second_w):
    width = merge.shape[0]
    for a in range(3):
        rows = slice(a * width, (a + 1) * width)
        for out, layer in ((first_w, 0), (second_w, 1)):
            out[rows] = res[0, layer, :, 3 * a * width : 3 * (a + 1) * width]
        for out, which in ((frame_w, 0), (warp_w, 1)):
            starts = [(2 * (3 * a + b) + which) * width for b in range(3)]
            out[rows] = jnp.concatenate([merge[:, s : s + width] for s in starts], axis=1)


def frame_kernel(tick, carry, frames, weight, _, part, *rest):
    (frame, sems) = rest[-2:]
    source = frames if len(frames.shape) == 3 else frames.at[0, tick]
    copy = pltpu.make_async_copy(source, frame, sems.at[0])
    copy.start()
    if carry:
        passed = pltpu.make_async_copy(frames.at[0, tick + 1], rest[0], sems.at[1])
        passed.start()
    copy.wait()
    even, odd = split_rows(jnp.swapaxes(frame[...], 0, 1))
    for g in range(part.shape[0]):
        part[g, 0], part[g, 1] = conv_block(even[g], odd[g], weight[...])
    if carry:
        passed.wait()


def advance(blocks, reads, part, warp_w, first_w, second_w, hidden):
    per_owner = part.shape[0]
    merged, middle = {}, {}

    def merge(g):
        warped = displaced(blocks.at[g], reads[2 * per_owner + g], reads[3 * per_owner + g])
        sums = conv_block(*warped, warp_w[...])
        sums = [part[g, h] + sums[h] for h in range(2)]
        merged[g] = [jnp.maximum(v, 0.1 * v).astype(BF16) for v in sums]

    def first(g):
        middle[g] = [
            jnp.maximum(v, 0.0).astype(BF16) for v in conv_block(*merged[g], first_w[...])
        ]

    def second(g):
        sums = conv_block(*middle[g], second_w[...])
        for h in range(2):
            hidden[g, h] = (merged[g][h].astype(F32) + sums[h]).astype(BF16)

    stages = (merge, first, second)
    groups = per_owner // GROUP
    for step in range(groups + len(stages) - 1):
        for at in reversed(range(len(stages))):
            if 0 <= step - at < groups:
                for g in range((step - at) * GROUP, (step - at + 1) * GROUP):
                    stages[at](g)


def tick_kernel(tiles, slots, halve, reads, sends_at, *rest):
    pools, (part, warp_w, first_w, second_w, hidden, token), rest = (
        rest[:tiles], rest[tiles : tiles + 6], rest[tiles + 6 :]
    )
    token[0] = 0
    sends, (blocks, sems, send_sems) = rest[:-3], rest[-3:]
    whole = slice(None)
    waited(gather_blocks([(pool, whole) for pool in pools], reads, lambda g: blocks.at[g], sems))
    advance(blocks, reads, part, warp_w, first_w, second_w, hidden)
    if halve:
        lower, *sends = sends
        half = lower.shape[2]
        copies = started(
            [pltpu.make_async_copy(hidden.at[:, :, pl.ds(0, half)], lower, sems.at[0])]
        )
        waited(copies + send_slots(hidden, sends_at, sends, slots, send_sems, pl.ds(half, half)))
    else:
        waited(send_slots(hidden, sends_at, sends, slots, send_sems))


def turn_kernel(tiles, slots, reads, sends_at, *rest):
    pools, (lower, _, _, upper), rest = rest[:tiles], rest[tiles : tiles + 4], rest[tiles + 4 :]
    sends, (sems, send_sems) = rest[:-2], rest[-2:]
    half = lower.shape[2]
    copies = send_slots(lower, sends_at, sends, slots, send_sems)
    parts = [(pool, pl.ds(half, half) if j == 0 else slice(None)) for j, pool in enumerate(pools)]
    waited(gather_blocks(parts, reads, lambda g: upper.at[g], sems))
    waited(copies)


def lay_out(hidden, channels):
    top, low = join_rows(hidden[:, 0, channels], hidden[:, 1, channels])
    return jnp.swapaxes(jnp.concatenate([top, low], axis=-1), 0, 1)


def last_kernel(tiles, reads, *rest):
    pools, (upper, part, warp_w, first_w, second_w, *home, _, out), rest = (
        rest[:tiles], rest[tiles : tiles + 9], rest[tiles + 9 :]
    )
    blocks, hidden, laid, sems, more_sems = rest
    half, ticks = upper.shape[2], out.shape[1]
    copies = started(
        [
            pltpu.make_async_copy(upper, blocks.at[:, :, pl.ds(half, half)], more_sems.at[0]),
            *(
                pltpu.make_async_copy(
                    moved,
                    out.at[0, ticks - 2, pl.ds(i * home[0].shape[0], moved.shape[0])],
                    more_sems.at[1 + i],
                )
                for i, moved in enumerate(home)
            ),
        ]
    )
    parts = [(pool, slice(None)) for pool in pools]
    waited(gather_blocks(parts, reads, lambda g: blocks.at[g, :, pl.ds(0, half)], sems))
    copies[0].wait()
    advance(blocks, reads, part, warp_w, first_w, second_w, hidden)
    chunk = laid.shape[0] // 4
    for i in range(4):
        at = slice(i * chunk, (i + 1) * chunk)
        laid[at] = lay_out(hidden, at)
        copies += started(
            [
                pltpu.make_async_copy(
                    laid.at[pl.ds(i * chunk, chunk)],
                    out.at[0, ticks - 1, pl.ds(i * chunk, chunk)],
                    more_sems.at[3 + i],
                )
            ]
        )
    waited(copies[1:])


def place_kernel(blocks, _, out, token, laid, sem):
    token[0] = 0
    laid[...] = lay_out(blocks, slice(None))
    waited(started([pltpu.make_async_copy(laid, out.at[0, 0], sem)]))


def hand_kernel(held, _, later, sem):
    waited(started([pltpu.make_async_copy(held, later, sem)]))


def lay_kernel(blocks, *laid):
    field, at = lay_out(blocks, slice(None)), 0
    for out in laid:
        out[...] = field[at : at + out.shape[0]]
        at += out.shape[0]


def spec(space):
    return pl.BlockSpec(memory_space=space)


def along(value, axis, steps):
    count = lax.axis_size(axis)
    return lax.ppermute(value, axis, [(s, (s + steps) % count) for s in range(count)])


def across_tiles(sends):
    count = lax.axis_size("tile")
    return [
        lax.ppermute(value, "tile", [(s, s ^ (j + 1)) for s in range(count)])
        for j, value in enumerate(sends)
    ]


def call(kernel, out_shape, in_spaces, out_spaces, scratch=(), aliases=None, room=VMEM_LIMIT):
    return pl.pallas_call(
        kernel,
        out_shape=out_shape,
        in_specs=[spec(space) for space in in_spaces],
        out_specs=[spec(space) for space in out_spaces],
        scratch_shapes=list(scratch),
        input_output_aliases=aliases or {},
        compiler_params=pltpu.CompilerParams(vmem_limit_bytes=room),
        cost_estimate=pl.CostEstimate(flops=1, bytes_accessed=1, transcendentals=0),
    )


def per_device(frames, state_in, motion, merge_w, res_w):
    tiles = lax.axis_size("tile")
    _, ticks, channels, per_owner, pixels = frames.shape
    slots = max(2, 2 * per_owner // tiles)
    half = channels // 2
    hbm, vmem, smem, main = pl.ANY, pltpu.VMEM, pltpu.SMEM, pltpu.HBM
    dma = pltpu.SemaphoreType.DMA

    def blocks_of(count, width=channels, kind=BF16):
        return jax.ShapeDtypeStruct((count, 2, width, pixels // 2), kind)

    motion = motion.transpose(0, 2, 1, 3)
    slot_count = (tiles - 1) * slots
    table_size = (tiles - 1) * (slots + 1)
    motion_scratch = [pltpu.SMEM((motion.shape[0], *motion.shape[2:]), jnp.int32), dma]
    square = jax.ShapeDtypeStruct((3 * channels, 3 * channels), BF16)
    laid_shape = (channels, per_owner, pixels)

    def tables(tick, ahead):
        return call(
            functools.partial(table_kernel, tiles, slots, tick, ahead),
            [
                jax.ShapeDtypeStruct((4 * per_owner,), jnp.int32),
                jax.ShapeDtypeStruct((table_size,), jnp.int32),
            ],
            [hbm, smem],
            [smem] * 2,
            [*motion_scratch, pltpu.SMEM((tiles,), jnp.int32)],
        )(motion, token)

    order = jax.ShapeDtypeStruct((8,), jnp.int32)
    own, token, *sends = call(
        functools.partial(first_kernel, tiles, slots),
        [blocks_of(per_owner), order] + [blocks_of(slots)] * (tiles - 1),
        [hbm, main],
        [vmem, smem] + [hbm] * (tiles - 1),
        [
            *motion_scratch,
            pltpu.SMEM((table_size,), jnp.int32),
            dma((slot_count,)),
            pltpu.VMEM(laid_shape, BF16),
            dma((4,)),
        ],
        room=FULL_VMEM,
    )(motion, state_in)
    arrived = across_tiles(sends)
    frame_w, *weights = call(
        weight_kernel, [square] * 4, [vmem] * 2 + [smem], [vmem] * 4
    )(merge_w, res_w, token)
    warp_w, first_w, second_w = weights
    table = [tables(tick, tick) for tick in range(ticks)]
    last_table = tables(ticks - 1, 0)
    source = frames
    for tick in range(ticks - 1):
        carry = tick + 2 < ticks
        part, *passed = call(
            functools.partial(frame_kernel, tick, carry),
            [blocks_of(per_owner, kind=F32)]
            + [jax.ShapeDtypeStruct(laid_shape, BF16)] * carry,
            [hbm if tick else main, vmem, smem],
            [vmem] + [hbm] * carry,
            [pltpu.VMEM(laid_shape, BF16), dma((2,))],
        )(source, frame_w, token)
        if carry:
            source = along(passed[0], "frame", -(tick + 1))
        halve = tick + 2 == ticks
        width = half if halve else channels
        hidden, token, *sends = call(
            functools.partial(tick_kernel, tiles, slots, halve),
            [blocks_of(per_owner), order]
            + [blocks_of(per_owner, half)] * halve
            + [blocks_of(slots, width)] * (tiles - 1),
            [smem] * 2 + [hbm] * tiles + [vmem] * 4,
            [vmem, smem] + [hbm] * (tiles - 1 + halve),
            [pltpu.VMEM(blocks_of(per_owner).shape, BF16), dma((per_owner,)), dma((slot_count,))],
        )(table[tick][0], table[tick + 1][1], own, *arrived, part, *weights)
        own = hidden
        if not halve:
            arrived = across_tiles(sends)
            early = hidden
    lower, *sends = sends
    lower = along(lower, "frame", ticks - 1)
    arrived = across_tiles(sends)
    later_count = 3 * channels // 8
    laid_parts = [
        jax.ShapeDtypeStruct((count, *laid_shape[1:]), BF16)
        for count in (channels - later_count, later_count)
    ]
    laid = call(lay_kernel, laid_parts, [vmem], [vmem] * 2)(own)
    home = [along(laid[0], "frame", ticks - 2)]
    last_part = call(
        functools.partial(frame_kernel, ticks - 1, False),
        [blocks_of(per_owner, kind=F32)],
        [main, vmem, smem],
        [vmem],
        [pltpu.VMEM(laid_shape, BF16), dma((2,))],
    )(frames, frame_w, token)[0]
    result, placed = call(
        place_kernel,
        [jax.ShapeDtypeStruct(frames.shape, BF16), order],
        [vmem, smem],
        [main, smem],
        [pltpu.VMEM(laid_shape, BF16), dma],
    )(early, token)
    upper, *sends = call(
        functools.partial(turn_kernel, tiles, slots),
        [blocks_of(per_owner, half)] + [blocks_of(slots, half)] * (tiles - 1),
        [smem] * 2 + [hbm] * (tiles + 2) + [smem],
        [hbm] * tiles,
        [dma((per_owner,)), dma((slot_count,))],
    )(table[-1][0], last_table[1], own, *arrived, lower, last_part, placed)
    moved_upper = along(upper, "frame", ticks - 1)
    arrived = across_tiles(sends)
    later = call(hand_kernel, laid_parts[1:], [hbm] * 2, [hbm], [dma])(laid[1], upper)[0]
    home.append(along(later, "frame", ticks - 2))
    return call(
        functools.partial(last_kernel, tiles),
        [jax.ShapeDtypeStruct(frames.shape, BF16)],
        [smem] + [hbm] * (tiles + 1) + [vmem] * 4 + [hbm] * 2 + [main],
        [main],
        [
            pltpu.VMEM(blocks_of(per_owner).shape, BF16),
            pltpu.VMEM(blocks_of(per_owner).shape, BF16),
            pltpu.VMEM(laid_shape, BF16),
            dma((per_owner,)),
            dma((7,)),
        ],
        aliases={tiles + 8: 0},
    )(last_table[0], lower, *arrived, moved_upper, last_part, *weights, *home, result)[0]


def solution(mesh):
    placed = (P("frame", None, None, "tile", None), P("frame", None, "tile", None), P(), P(), P())
    return jax.shard_map(
        per_device,
        mesh=mesh,
        in_specs=placed,
        out_specs=P("frame", None, None, "tile", None),
        check_vma=False,
    )
```
